32 devices in a mesh: ctx: 16 (over z, y, x), head: 2 (over core).
Axes of the slice: x: 2, y: 2, z: 4, core: 2. Of those that a mesh axis runs over, the one named last changes fastest.
Arguments:
- queries: bfloat16 [4096, 1024], P('ctx', 'head'), may hold values from -10 to 10
- keys: bfloat16 [4096, 128], P('ctx'), may hold values from -6 to 6
- values: bfloat16 [4096, 128], P('ctx'), may hold values from -6 to 6
- doc_lengths: int32 [4], replicated, may hold values from 1 to 3072, 4096 in all
Outputs:
- attn_rows: bfloat16 [4096, 1024], P('ctx', 'head')
- col_scores: float32 [4096], P(('ctx', 'head'))
The draws below stay inside these ranges and needn't reach their ends.
Inputs may be any that keep to these rules, and one draw needn't show every extreme that they name: `doc_lengths`: the 4 lengths sum to 4096 and the longest is exactly 3072.
All inputs are finite; a program needn't handle non-finite values.
Results may differ from the reference program's by a relative error of at most 0.0075.
Values may be sent and summed in bfloat16 or wider, within the bound.
A program may use at most 64 MiB of HBM per device.

```python
import math
import jax
import jax.numpy as jnp
import numpy as np
from jax import lax

HD = 128
HEADS = 8
SEQS = 4
TOK_DEV = 256
TOKENS = 4096


def draw_queries(key, part):
    key = jax.random.fold_in(key, 11)
    result = 2.5 * jax.random.truncated_normal(key, -4.0, 4.0, (TOKENS, HEADS * HD))
    return result.astype(jnp.float32).astype(jnp.bfloat16)


def draw_keys(key, part):
    key = jax.random.fold_in(key, 23)
    result = jax.random.truncated_normal(key, -6.0, 6.0, (TOKENS, HD))
    return result.astype(jnp.float32).astype(jnp.bfloat16)


def levels(key, extent, cuts, smallest, largest):
    gain, own = 1.0, jax.random.fold_in(key, 6)
    for position, blocks in cuts:
        heights = jnp.exp(jax.random.uniform(jax.random.fold_in(own, position), (blocks,), jnp.float32, smallest / len(cuts), largest / len(cuts)))
        gain = gain * jnp.repeat(heights, extent[position] // blocks).reshape([-1 if axis == position else 1 for axis in range(len(extent))])
    return gain


def split_up(count, total, reach, lean):
    portions = [(1 << 20) // math.isqrt(rank ** lean) + 1 for rank in range(2, count + 1)]
    rest, counts = total - reach - (count - 1), [1] * (count - 1)
    while rest > 0:
        movable = [i for i in range(count - 1) if counts[i] < reach]
        whole, remaining = sum([portions[i] for i in movable]), rest
        for i in movable:
            more = min(reach - counts[i], max(1, remaining * portions[i] // whole), rest)
            counts[i] = counts[i] + more
            rest = rest - more
    return np.array([reach] + counts)


def uneven(own_key, amount, total, bound, skew):
    if amount == 2:
        one = jax.random.randint(own_key, (), max(1, total - bound), min(bound, total - 1) + 1)
        return jnp.stack([one, total - one])
    sizes = jnp.asarray(split_up(amount, total, bound, skew), jnp.int32)
    twos = (amount - 1) // 2
    source_of, taker = sizes[1:1 + 2 * twos:2], sizes[2:2 + 2 * twos:2]
    slack = jnp.minimum(source_of - 1, bound - taker)
    shifted = jax.random.randint(jax.random.fold_in(own_key, 1), (twos,), 0, 1 << 20) % (slack + 1)
    sizes = sizes.at[1:1 + 2 * twos:2].set(source_of - shifted).at[2:2 + 2 * twos:2].set(taker + shifted)
    return sizes[jax.random.permutation(jax.random.fold_in(own_key, 2), amount)]


def gaussian(stream_key, extent, scale, reach, shards=(), held_as=jnp.bfloat16):
    gain = levels(stream_key, extent, shards, -0.22, 0.18) if shards else 1.0
    values = jax.random.normal(stream_key, extent, jnp.float32) * scale * gain
    return jnp.minimum(jnp.maximum(values, -reach), reach).astype(held_as)


def setup_inputs(seed: int = 0) -> dict:
    key_list = jax.random.split(jax.random.key(seed), 5)
    queries = draw_queries(jax.random.fold_in(key_list[4], 71), 0)
    keys = draw_keys(jax.random.fold_in(key_list[4], 71), 0)
    values = gaussian(key_list[2], (TOKENS, HD), 1.0, 6.0, ((0, 16),))
    doc_lengths = uneven(key_list[3], SEQS, TOKENS, 3 * TOKENS // 4, 2).astype(jnp.int32)
    return {"queries": queries, "keys": keys, "values": values, "doc_lengths": doc_lengths}


def doc_index(doc_lengths, positions):
    doc_ends = jnp.cumsum(doc_lengths)
    return lax.optimization_barrier(jnp.sum((positions[:, None] >= doc_ends[None, :]).astype(jnp.int32), axis=1))

def reference(queries, keys, values, doc_lengths):
    inv_root = 1.0 / math.sqrt(HD)
    positions = jnp.arange(TOKENS, dtype=jnp.int32)
    key_docs = doc_index(doc_lengths, positions)
    per_block = queries.reshape(TOKENS // TOK_DEV, TOK_DEV, HEADS, HD)

    def one_block(block_index):
        q_block = per_block[block_index]
        q_pos = block_index * TOK_DEV + jnp.arange(TOK_DEV, dtype=jnp.int32)
        q_docs = doc_index(doc_lengths, q_pos)
        allowed = (key_docs[None, :] == q_docs[:, None]) & (positions[None, :] <= q_pos[:, None])

        def one_head(head_index):
            q_rows = q_block[:, head_index, :]
            logits = jnp.dot(q_rows, keys.T, preferred_element_type=jnp.float32) * inv_root
            logits = jnp.where(allowed, logits, -jnp.inf)
            row_max = lax.optimization_barrier(jnp.max(logits, axis=1, keepdims=True))
            log_norm = row_max + jnp.log(lax.optimization_barrier(jnp.sum(jnp.exp(logits - row_max), axis=1, keepdims=True)))
            probs = jnp.exp(logits - log_norm)
            rows_out = jnp.dot(probs.astype(jnp.bfloat16), values, preferred_element_type=jnp.float32).astype(jnp.bfloat16)
            return (rows_out, lax.optimization_barrier(jnp.sum(probs, axis=0)))
        head_rows, head_cols = lax.map(one_head, jnp.arange(HEADS, dtype=jnp.int32))
        return (head_rows, lax.optimization_barrier(jnp.sum(head_cols, axis=0)))
    block_rows, block_cols = lax.map(one_block, jnp.arange(TOKENS // TOK_DEV, dtype=jnp.int32))
    attn_rows = block_rows.transpose(0, 2, 1, 3).reshape(TOKENS, HEADS * HD)
    col_scores = lax.optimization_barrier(jnp.sum(block_cols, axis=0)) / HEADS
    return (attn_rows, col_scores)
```

```python
import functools
import math

import jax
import jax.numpy as jnp
from jax import lax
from jax.experimental import pallas as pl
from jax.experimental.pallas import tpu as pltpu
from jax.sharding import PartitionSpec as P

HD = 128
HEADS = 8
PLANE = 4
BIG = 32768.0
MESH = pl.DeviceIdType.MESH
SCALE = math.log2(math.e) / math.sqrt(HD)


def place(planes):
    me, core = lax.axis_index("ctx"), lax.axis_index("head")
    return me, core, me // PLANE, me % PLANE


def remote(src, dst, send, recv, ctx, core):
    return pltpu.make_async_remote_copy(
        src_ref=src,
        dst_ref=dst,
        send_sem=send,
        recv_sem=recv,
        device_id={"ctx": ctx, "head": core},
        device_id_type=MESH,
    )


class Gather:
    def __init__(self, planes, cores, kv, send, recv, sib_send, sib_recv):
        self.planes, self.cores, self.kv = planes, cores, kv
        self.send, self.recv = send, recv
        self.sib_send, self.sib_recv = sib_send, sib_recv
        self.me, self.core, self.z, self.p = place(planes)
        self.px = self.p + 1 - 2 * (self.p % 2)
        self.py = (self.p + 2) % PLANE
        self.pd = (self.px + 2) % PLANE
        self.xn = self.z * PLANE + self.px
        self.yn = self.z * PLANE + self.py

    def block(self, s, which):
        return (self.z - s) * PLANE + (self.p, self.px, self.py, self.pd)[which]

    def ref(self, s, kind, core):
        if kind < 3:
            return self.kv.at[self.block(s, kind), core]
        return self.kv.at[self.block(s, 3), core, 4 - kind]

    def chain_copy(self, s):
        ref = self.ref(s, 0, self.core)
        return remote(ref, ref, self.send.at[0, s], self.recv.at[0, s + 1], self.me + PLANE, self.core)

    def plane_copy(self, s, kind):
        ref = self.ref(s, 0, self.core)
        if kind == 3:
            ref = self.kv.at[self.block(s, 1), self.core, 1]
        if kind == 4:
            ref = self.kv.at[self.block(s, 2), self.core, 0]
        to = self.xn if kind in (1, 4) else self.yn
        return remote(ref, ref, self.send.at[kind, s], self.recv.at[kind, s], to, self.core)

    def sib_copy(self, s, kind, step):
        ref = self.ref(s, kind, self.core)
        return remote(
            ref,
            ref,
            self.sib_send.at[kind, step - 1, s],
            self.sib_recv.at[kind, step - 1, s],
            self.me,
            (self.core + step) % self.cores,
        )

    def wait_arrival(self, s, kind):
        ref = self.ref(s, kind, self.core)
        remote(ref, ref, self.send.at[kind, s], self.recv.at[kind, s], self.xn, self.core).wait_recv()

    def sibs(self, s, kind):
        if kind == 0 and s == 0:
            return
        for step in range(1, self.cores):
            self.sib_copy(s, kind, step).start()

    def barrier(self):
        sem = pltpu.get_barrier_semaphore()

        def tell(ctx, core):
            pl.semaphore_signal(sem, inc=1, device_id={"ctx": ctx, "head": core}, device_id_type=MESH)

        tell(self.xn, self.core)
        tell(self.yn, self.core)
        for step in range(1, self.cores):
            tell(self.me, (self.core + step) % self.cores)
        pl.when(self.z > 0)(lambda: tell(self.me - PLANE, self.core))
        pl.when(self.z < self.planes - 1)(lambda: tell(self.me + PLANE, self.core))
        ends = (self.z > 0).astype(jnp.int32) + (self.z < self.planes - 1).astype(jnp.int32)
        pl.semaphore_wait(sem, 1 + self.cores + ends)

    def chain(self, s):
        @pl.when(s <= self.z)
        def _():
            if s > 0:
                self.wait_arrival(s, 0)
            if s < self.planes - 1:
                pl.when(self.z < self.planes - 1)(lambda: self.chain_copy(s).start())
            self.plane_copy(s, 1).start()
            self.plane_copy(s, 2).start()
            self.sibs(s, 0)

    def cross(self, s):
        @pl.when(s <= self.z)
        def _():
            self.wait_arrival(s, 1)
            self.plane_copy(s, 3).start()
            self.sibs(s, 1)
            self.wait_arrival(s, 2)
            self.plane_copy(s, 4).start()
            self.sibs(s, 2)

    def diagonal(self, s):
        @pl.when(s <= self.z)
        def _():
            for kind in (3, 4):
                self.wait_arrival(s, kind)
                self.sibs(s, kind)

    def landed(self, s):
        @pl.when(s <= self.z)
        def _():
            for kind in range(5):
                if kind == 0 and s == 0:
                    continue
                for step in range(1, self.cores):
                    ref = self.ref(s, kind, (self.core + self.cores - step) % self.cores)
                    remote(
                        ref,
                        ref,
                        self.sib_send.at[kind, step - 1, s],
                        self.sib_recv.at[kind, step - 1, s],
                        self.me,
                        (self.core + step) % self.cores,
                    ).wait_recv()

    def sent(self, s):
        @pl.when(s <= self.z)
        def _():
            if s < self.planes - 1:
                pl.when(self.z < self.planes - 1)(lambda: self.chain_copy(s).wait_send())
            for kind in range(5):
                if kind > 0:
                    self.plane_copy(s, kind).wait_send()
                if kind == 0 and s == 0:
                    continue
                for step in range(1, self.cores):
                    self.sib_copy(s, kind, step).wait_send()


def gather_sems(planes, cores):
    return [
        pltpu.SemaphoreType.DMA((5, planes)),
        pltpu.SemaphoreType.DMA((5, planes)),
        pltpu.SemaphoreType.DMA((5, max(cores - 1, 1), planes)),
        pltpu.SemaphoreType.DMA((5, max(cores - 1, 1), planes)),
    ]


def gather_kernel(planes, cores, k_ref, v_ref, kv, *sems):
    g = Gather(planes, cores, kv, *sems)
    width = kv.shape[3]
    for part in range(cores):
        rows = pl.ds(part * width, width)
        kv[g.me, part, 0] = k_ref[rows, :]
        kv[g.me, part, 1] = v_ref[rows, :]
    g.barrier()
    for t in range(planes + 2):
        if t < planes:
            g.chain(t)
        if 0 <= t - 1 < planes:
            g.cross(t - 1)
        if 0 <= t - 2:
            g.diagonal(t - 2)
    for s in range(planes):
        g.landed(s)
    for s in range(planes):
        g.sent(s)


def doc_of(ends, start, shape):
    position = start + lax.broadcasted_iota(jnp.int32, shape, 0)
    result = jnp.zeros(shape, jnp.int32)
    for end in ends:
        result += (position >= end).astype(jnp.int32)
    return result


def attend_kernel(planes, cores, docs_ref, q_ref, kv, out_ref, cols_ref, qx, s_ref, p_ref, m_ref, acc):
    me = lax.axis_index("ctx")
    tok, heads = q_ref.shape[0], q_ref.shape[1] // HD
    width = kv.shape[3]
    ends, total = [], 0
    for i in range(docs_ref.shape[0]):
        total = total + docs_ref[i]
        ends.append(total)
    first = jnp.int32(0)
    for end in ends:
        first = jnp.where(end <= me * tok, end, first)
    low = first // tok

    lane = lax.broadcasted_iota(jnp.int32, (tok, HD), 1)
    mark = jnp.where(lane == doc_of(ends, me * tok, (tok, HD)), 1.0, 0.0).astype(jnp.bfloat16)
    for h in range(heads):
        qx[h, :, :HD] = q_ref[:, h * HD : (h + 1) * HD]
        qx[h, :, HD:] = mark

    def part(b, which):
        return jnp.concatenate([kv[b, c, which] for c in range(cores)], axis=0)

    def logits(b, h, kx):
        return lax.dot_general(qx[h], kx, (((1,), (1,)), ((), ())), preferred_element_type=jnp.float32)

    def wide_keys(b):
        bar = jnp.where(lane == doc_of(ends, b * tok, (tok, HD)), 0.0, -BIG).astype(jnp.bfloat16)
        return jnp.concatenate([part(b, 0), bar], axis=1)

    def halves(x, op):
        result = x[:, :HD]
        for i in range(1, x.shape[1] // HD):
            result = op(result, x[:, i * HD : (i + 1) * HD])
        return result

    row = lax.broadcasted_iota(jnp.int32, (tok, tok), 0)
    col = lax.broadcasted_iota(jnp.int32, (tok, tok), 1)
    kx = wide_keys(me)
    for h in range(heads):
        s = jnp.where(col <= row, logits(me, h, kx), -BIG)
        s_ref[me, h] = s
        m_ref[h] = halves(s, jnp.maximum)

    def scan(b, carry):
        kx = wide_keys(b)
        for h in range(heads):
            s = logits(b, h, kx)
            s_ref[b, h] = s
            m_ref[h] = jnp.maximum(m_ref[h], halves(s, jnp.maximum))
        return carry

    lax.fori_loop(low, me, scan, 0)
    for h in range(heads):
        top = jnp.max(m_ref[h], axis=1, keepdims=True) * SCALE
        m_ref[h] = jnp.broadcast_to(top, (tok, HD))
    acc[...] = jnp.zeros_like(acc)
    ones = jnp.ones((tok, HD), jnp.bfloat16)

    def weigh(b, carry):
        vx = jnp.concatenate([part(b, 1), ones], axis=1)
        for h in range(heads):
            m = m_ref[h]
            p = jnp.exp2(s_ref[b, h] * SCALE - jnp.concatenate([m] * (tok // HD), axis=1))
            p = p.astype(jnp.bfloat16)
            p_ref[b, h] = p
            acc[h] += jnp.dot(p, vx, preferred_element_type=jnp.float32)
        return carry

    lax.fori_loop(low, me + 1, weigh, 0)
    weights = []
    line = lax.broadcasted_iota(jnp.int32, (16, tok), 0)
    for h in range(heads):
        inverse = 1.0 / acc[h, :, HD:]
        out_ref[:, h * HD : (h + 1) * HD] = (acc[h, :, :HD] * inverse).astype(out_ref.dtype)
        across = jnp.transpose(inverse)[:16]
        high = across.astype(jnp.bfloat16)
        rest = (across - high.astype(jnp.float32)).astype(jnp.bfloat16)
        none = jnp.zeros_like(high)
        weights.append(jnp.where(line == 0, high, jnp.where(line == 1, rest, none)))
    cols_ref[...] = jnp.zeros_like(cols_ref)

    def columns(b, carry):
        sums = jnp.zeros((16, tok), jnp.float32)
        for h in range(heads):
            sums += jnp.dot(weights[h], p_ref[b, h], preferred_element_type=jnp.float32)
        sums = jnp.sum(sums, axis=0, keepdims=True)
        for c in range(cores):
            cols_ref[b % PLANE, c, b // PLANE] = sums[:, c * width : (c + 1) * width]
        return carry

    lax.fori_loop(low, me + 1, columns, 0)


def reduce_kernel(planes, cores, cols_ref, out_ref, held, mid, late, send, recv, zsend, zrecv):
    me, core, z, p = place(planes)
    sem = pltpu.get_barrier_semaphore()
    steps = [(a, c) for a in range(PLANE) for c in range(cores) if (a, c) != (0, 0)]

    def tell(ctx, to):
        pl.semaphore_signal(sem, inc=1, device_id={"ctx": ctx, "head": to}, device_id_type=MESH)

    for a, c in steps:
        tell(z * PLANE + (p + a) % PLANE, (core + c) % cores)
    for step in range(1, planes):
        tell((z + step) % planes * PLANE + p, core)
    pl.semaphore_wait(sem, len(steps) + planes - 1)

    def plane_copy(n):
        a, c = steps[n]
        pn, cn = (p + a) % PLANE, (core + c) % cores
        return remote(cols_ref.at[pn, cn], held.at[n], send.at[n], recv.at[n], z * PLANE + pn, cn)

    for n in range(len(steps)):
        plane_copy(n).start()
    total = cols_ref[p, core]
    for n in range(len(steps)):
        plane_copy(n).wait_recv()
        total += held[n]
    mid[...] = total

    def z_copy(step):
        to = (z + step) % planes
        return remote(mid.at[to], late.at[step], zsend.at[step], zrecv.at[step], to * PLANE + p, core)

    for step in range(1, planes):
        z_copy(step).start()
    result = mid[z]
    for step in range(1, planes):
        z_copy(step).wait_recv()
        result += late[step]
    out_ref[...] = result * (1.0 / HEADS)
    for n in range(len(steps)):
        plane_copy(n).wait_send()
    for step in range(1, planes):
        z_copy(step).wait_send()


def body(planes, cores, queries, keys, values, doc_lengths):
    tok, heads = queries.shape[0], queries.shape[1] // HD
    ctx, width = planes * PLANE, tok // cores
    vmem = pl.BlockSpec(memory_space=pltpu.VMEM)
    limit = 48 * 1024 * 1024
    kv = pl.pallas_call(
        functools.partial(gather_kernel, planes, cores),
        out_shape=jax.ShapeDtypeStruct((ctx, cores, 2, width, HD), jnp.bfloat16),
        in_specs=[vmem] * 2,
        out_specs=vmem,
        scratch_shapes=gather_sems(planes, cores),
        compiler_params=pltpu.CompilerParams(collective_id=0, has_side_effects=True, vmem_limit_bytes=limit),
        name="gather",
    )(keys, values)
    rows, cols = pl.pallas_call(
        functools.partial(attend_kernel, planes, cores),
        out_shape=(
            jax.ShapeDtypeStruct(queries.shape, jnp.bfloat16),
            jax.ShapeDtypeStruct((PLANE, cores, planes, 1, width), jnp.float32),
        ),
        in_specs=[pl.BlockSpec(memory_space=pltpu.SMEM), vmem, vmem],
        out_specs=(vmem, vmem),
        scratch_shapes=[
            pltpu.VMEM((heads, tok, 2 * HD), jnp.bfloat16),
            pltpu.VMEM((ctx, heads, tok, tok), jnp.float32),
            pltpu.VMEM((ctx, heads, tok, tok), jnp.bfloat16),
            pltpu.VMEM((heads, tok, HD), jnp.float32),
            pltpu.VMEM((heads, tok, 2 * HD), jnp.float32),
        ],
        compiler_params=pltpu.CompilerParams(vmem_limit_bytes=limit),
        name="attend",
    )(doc_lengths, queries, kv)
    partners = PLANE * cores - 1
    scores = pl.pallas_call(
        functools.partial(reduce_kernel, planes, cores),
        out_shape=jax.ShapeDtypeStruct((1, width), jnp.float32),
        in_specs=[vmem],
        out_specs=vmem,
        scratch_shapes=[
            pltpu.VMEM((partners, planes, 1, width), jnp.float32),
            pltpu.VMEM((planes, 1, width), jnp.float32),
            pltpu.VMEM((planes, 1, width), jnp.float32),
            pltpu.SemaphoreType.DMA((partners,)),
            pltpu.SemaphoreType.DMA((partners,)),
            pltpu.SemaphoreType.DMA((planes,)),
            pltpu.SemaphoreType.DMA((planes,)),
        ],
        compiler_params=pltpu.CompilerParams(collective_id=1, has_side_effects=True),
        name="reduce",
    )(cols)
    return rows, scores.reshape(width)


def solution(mesh):
    planes, cores = mesh.shape["ctx"] // PLANE, mesh.shape["head"]
    return jax.shard_map(
        functools.partial(body, planes, cores),
        mesh=mesh,
        in_specs=(P("ctx", "head"), P("ctx", None), P("ctx", None), P()),
        out_specs=(P("ctx", "head"), P(("ctx", "head"))),
        check_vma=False,
    )
```

```python
import functools
import math

import jax
import jax.numpy as jnp
from jax import lax
from jax.experimental import pallas as pl
from jax.experimental.pallas import tpu as pltpu
from jax.sharding import PartitionSpec as P

HD = 128
HEADS = 8
PLANE = 4
BIG = 32768.0
MESH = pl.DeviceIdType.MESH
SCALE = math.log2(math.e) / math.sqrt(HD)


def place(planes):
    me, core = lax.axis_index("ctx"), lax.axis_index("head")
    return me, core, me // PLANE, me % PLANE


def remote(src, dst, send, recv, ctx, core):
    return pltpu.make_async_remote_copy(
        src_ref=src,
        dst_ref=dst,
        send_sem=send,
        recv_sem=recv,
        device_id={"ctx": ctx, "head": core},
        device_id_type=MESH,
    )


class Gather:
    def __init__(self, planes, cores, kv, send, recv, sib_send, sib_recv):
        self.planes, self.cores, self.kv = planes, cores, kv
        self.send, self.recv = send, recv
        self.sib_send, self.sib_recv = sib_send, sib_recv
        self.me, self.core, self.z, self.p = place(planes)
        self.px = self.p + 1 - 2 * (self.p % 2)
        self.py = (self.p + 2) % PLANE
        self.pd = (self.px + 2) % PLANE
        self.xn = self.z * PLANE + self.px
        self.yn = self.z * PLANE + self.py

    def block(self, s, which):
        return (self.z - s) * PLANE + (self.p, self.px, self.py, self.pd)[which]

    def ref(self, s, kind, core):
        if kind < 3:
            return self.kv.at[self.block(s, kind), core]
        return self.kv.at[self.block(s, 3), core, 4 - kind]

    def chain_copy(self, s):
        ref = self.ref(s, 0, self.core)
        return remote(ref, ref, self.send.at[0, s], self.recv.at[0, s + 1], self.me + PLANE, self.core)

    def plane_copy(self, s, kind):
        ref = self.ref(s, 0, self.core)
        if kind == 3:
            ref = self.kv.at[self.block(s, 1), self.core, 1]
        if kind == 4:
            ref = self.kv.at[self.block(s, 2), self.core, 0]
        to = self.xn if kind in (1, 4) else self.yn
        return remote(ref, ref, self.send.at[kind, s], self.recv.at[kind, s], to, self.core)

    def sib_copy(self, s, kind, step):
        ref = self.ref(s, kind, self.core)
        return remote(
            ref,
            ref,
            self.sib_send.at[kind, step - 1, s],
            self.sib_recv.at[kind, step - 1, s],
            self.me,
            (self.core + step) % self.cores,
        )

    def wait_arrival(self, s, kind):
        ref = self.ref(s, kind, self.core)
        remote(ref, ref, self.send.at[kind, s], self.recv.at[kind, s], self.xn, self.core).wait_recv()

    def sibs(self, s, kind):
        for step in range(1, self.cores):
            self.sib_copy(s, kind, step).start()

    def chain(self, s, own=False):
        @pl.when(s <= self.z)
        def _():
            if not own:
                self.wait_arrival(s, 0)
            pl.when(self.z < self.planes - 1)(lambda: self.chain_copy(s).start())
            self.plane_copy(s, 1).start()
            self.plane_copy(s, 2).start()
            if not own:
                self.sibs(s, 0)

    def cross(self, s):
        @pl.when(s <= self.z)
        def _():
            self.wait_arrival(s, 1)
            self.plane_copy(s, 3).start()
            self.sibs(s, 1)
            self.wait_arrival(s, 2)
            self.plane_copy(s, 4).start()
            self.sibs(s, 2)

    def diagonal(self, s):
        @pl.when(s <= self.z)
        def _():
            for kind in (4, 3):
                self.wait_arrival(s, kind)
                self.sibs(s, kind)

    def landed(self, s, kind):
        for step in range(1, self.cores):
            ref = self.ref(s, kind, (self.core + self.cores - step) % self.cores)
            remote(
                ref,
                ref,
                self.sib_send.at[kind, step - 1, s],
                self.sib_recv.at[kind, step - 1, s],
                self.me,
                (self.core + step) % self.cores,
            ).wait_recv()

    def sent(self, s, own=False):
        pl.when(self.z < self.planes - 1)(lambda: self.chain_copy(s).wait_send())
        for kind in range(5):
            if kind > 0:
                self.plane_copy(s, kind).wait_send()
            if kind > 0 or not own:
                for step in range(1, self.cores):
                    self.sib_copy(s, kind, step).wait_send()


def gather_sems(planes, cores):
    return [
        pltpu.SemaphoreType.DMA((5, planes)),
        pltpu.SemaphoreType.DMA((5, planes)),
        pltpu.SemaphoreType.DMA((5, max(cores - 1, 1), planes)),
        pltpu.SemaphoreType.DMA((5, max(cores - 1, 1), planes)),
    ]


def doc_of(ends, start, shape):
    position = start + lax.broadcasted_iota(jnp.int32, shape, 0)
    result = jnp.zeros(shape, jnp.int32)
    for end in ends:
        result += (position >= end).astype(jnp.int32)
    return result


def kernel(planes, cores, docs_ref, q_hbm, k_hbm, v_hbm, rows_hbm, out_ref, *scratch):
    q_ref, kv, qx, s_ref, p_ref, mx_ref, m_ref, acc, o_ref, comb, cols_ref, held, mid, late = scratch[:14]
    load, store, send, recv, zsend, zrecv = scratch[14:20]
    g = Gather(planes, cores, kv, *scratch[20:])
    me, core, z, p = g.me, g.core, g.z, g.p
    tok, heads = q_ref.shape[0], q_ref.shape[1] // HD
    width = tok // cores
    span = PLANE * tok
    steps = [(a, c) for a in range(PLANE) for c in range(cores) if (a, c) != (0, 0)]

    loads = [pltpu.make_async_copy(q_hbm, q_ref, load.at[2 * cores])]
    for part in range(cores):
        rows = pl.ds(part * width, width)
        loads.append(pltpu.make_async_copy(k_hbm.at[rows], kv.at[me, part, 0], load.at[2 * part]))
        loads.append(pltpu.make_async_copy(v_hbm.at[rows], kv.at[me, part, 1], load.at[2 * part + 1]))
    for copy in loads[1:] + loads[:1]:
        copy.start()

    sem = pltpu.get_barrier_semaphore()

    def tell(ctx, to):
        pl.semaphore_signal(sem, inc=1, device_id={"ctx": ctx, "head": to}, device_id_type=MESH)

    for a, c in steps:
        tell(z * PLANE + (p + a) % PLANE, (core + c) % cores)
    for step in range(1, planes):
        tell((z + step) % planes * PLANE + p, core)
    for copy in loads[1:]:
        copy.wait()
    pl.semaphore_wait(sem, len(steps) + planes - 1)
    g.chain(0, own=True)

    ends, total = [], 0
    for i in range(docs_ref.shape[0]):
        total = total + docs_ref[i]
        ends.append(total)
    lane = lax.broadcasted_iota(jnp.int32, (tok, HD), 1)
    mark = jnp.where(lane == doc_of(ends, me * tok, (tok, HD)), 1.0, 0.0).astype(jnp.bfloat16)
    loads[0].wait()
    for h in range(heads):
        qx[h, :, :HD] = q_ref[:, h * HD : (h + 1) * HD]
        qx[h, :, HD:] = mark
    cols_ref[...] = jnp.zeros_like(cols_ref)
    comb[...] = jnp.zeros_like(comb)
    ones = jnp.ones((tok, HD), jnp.bfloat16)
    row = lax.broadcasted_iota(jnp.int32, (tok, tok), 0)
    col = lax.broadcasted_iota(jnp.int32, (tok, tok), 1)

    def whole(b, which):
        return jnp.concatenate([kv[b, c, which] for c in range(cores)], axis=0)

    def scan(s, which, own):
        b = g.block(s, which)
        bar = jnp.where(lane == doc_of(ends, b * tok, (tok, HD)), 0.0, -BIG).astype(jnp.bfloat16)
        kx = jnp.concatenate([whole(b, 0), bar], axis=1)
        for h in range(heads):
            x = lax.dot_general(qx[h], kx, (((1,), (1,)), ((), ())), preferred_element_type=jnp.float32)
            if own:
                x = jnp.where(col + (b - me) * tok <= row, x, -BIG)
            s_ref[h, :, which * tok : (which + 1) * tok] = x
            top = x[:, :HD]
            for i in range(1, tok // HD):
                top = jnp.maximum(top, x[:, i * HD : (i + 1) * HD])
            mx_ref[h] = top if which == 0 else jnp.maximum(mx_ref[h], top)

    def weigh(s, h, own):
        top = jnp.broadcast_to(jnp.max(mx_ref[h], axis=1, keepdims=True) * SCALE, (tok, HD))
        if not own:
            old = m_ref[s - 1, h]
            top = jnp.maximum(old, top)
            fade = jnp.exp2(old - top)
        m_ref[s, h] = top
        wide = jnp.concatenate([top] * (tok // HD), axis=1)
        for which in range(PLANE):
            part = slice(which * tok, (which + 1) * tok)
            p_ref[s, h, :, part] = jnp.exp2(s_ref[h, :, part] * SCALE - wide).astype(jnp.bfloat16)
        vx = jnp.concatenate(
            [jnp.concatenate([whole(g.block(s, which), 1), ones], axis=1) for which in range(PLANE)], axis=0
        )
        new = jnp.dot(p_ref[s, h], vx, preferred_element_type=jnp.float32)
        if not own:
            new += acc[h] * jnp.concatenate([fade, fade], axis=1)
        acc[h] = new

    def one_round(s, own):
        if not own:
            g.landed(s, 0)
            scan(s, 0, own)
        g.landed(s, 1)
        scan(s, 1, own)
        g.chain(s + 2)
        g.landed(s, 2)
        scan(s, 2, own)
        g.cross(s + 1)
        g.landed(s, 4)
        g.landed(s, 3)
        scan(s, 3, own)
        for h in range(heads):
            weigh(s, h, own)
            if h == heads // 2:
                g.diagonal(s + 1)

    scan(0, 0, True)
    g.chain(1)
    g.cross(0)
    g.diagonal(0)
    one_round(0, True)

    @pl.loop(1, z + 1)
    def _(s):
        one_round(s, False)

    for h in range(heads):
        inverse = 1.0 / acc[h, :, HD:]
        o_ref[:, h * HD : (h + 1) * HD] = (acc[h, :, :HD] * inverse).astype(o_ref.dtype)
        acc[h, :, HD:] = inverse

    @pl.loop(0, z + 1)
    def _(s):
        for h in range(heads):
            weight = jnp.exp2(m_ref[s, h] - m_ref[z, h]) * acc[h, :, HD:]
            comb[...] = jnp.where(lane == s * heads + h, weight, comb[...])

    out_copy = pltpu.make_async_copy(o_ref, rows_hbm, store.at[0])
    out_copy.start()
    across = jnp.transpose(comb[...])
    held_rows = mx_ref
    for half in range(tok // HD):
        held_rows[0, half * HD : (half + 1) * HD, :] = across[:, half * HD : (half + 1) * HD]
    line = lax.broadcasted_iota(jnp.int32, (16, tok), 0)

    @pl.loop(0, z + 1)
    def _(s):
        sums = jnp.zeros((16, span), jnp.float32)
        for h in range(heads):
            w = jnp.concatenate(
                [held_rows[0, pl.ds(half * HD + s * heads + h, 1), :] for half in range(tok // HD)], axis=1
            )
            w = jnp.broadcast_to(w, (16, tok))
            high = w.astype(jnp.bfloat16).astype(jnp.float32)
            w = jnp.where(line == 0, high, jnp.where(line == 1, w - high, 0.0)).astype(jnp.bfloat16)
            sums += jnp.dot(w, p_ref[s, h], preferred_element_type=jnp.float32)
        sums = jnp.sum(sums, axis=0, keepdims=True)
        for which in range(PLANE):
            b = g.block(s, which)
            for c in range(cores):
                start = which * tok + c * width
                cols_ref[b % PLANE, c, b // PLANE] = sums[:, start : start + width]

    def plane_copy(n):
        a, c = steps[n]
        pn, cn = (p + a) % PLANE, (core + c) % cores
        return remote(cols_ref.at[pn, cn], held.at[n], send.at[n], recv.at[n], z * PLANE + pn, cn)

    for n in range(len(steps)):
        plane_copy(n).start()
    g.sent(0, own=True)

    @pl.loop(1, z + 1)
    def _(s):
        g.sent(s)

    total = cols_ref[p, core]
    for n in range(len(steps)):
        plane_copy(n).wait_recv()
        total += held[n]
    mid[...] = total

    def z_copy(step):
        to = (z + step) % planes
        return remote(mid.at[to], late.at[step], zsend.at[step], zrecv.at[step], to * PLANE + p, core)

    for step in range(1, planes):
        z_copy(step).start()
    result = mid[z]
    for step in range(1, planes):
        z_copy(step).wait_recv()
        result += late[step]
    out_ref[...] = result * (1.0 / HEADS)
    for n in range(len(steps)):
        plane_copy(n).wait_send()
    for step in range(1, planes):
        z_copy(step).wait_send()
    out_copy.wait()


def body(planes, cores, queries, keys, values, doc_lengths):
    tok, heads = queries.shape[0], queries.shape[1] // HD
    ctx, width = planes * PLANE, tok // cores
    partners = PLANE * cores - 1
    anywhere = pl.BlockSpec(memory_space=pl.ANY)
    rows, scores = pl.pallas_call(
        functools.partial(kernel, planes, cores),
        out_shape=(
            jax.ShapeDtypeStruct(queries.shape, jnp.bfloat16),
            jax.ShapeDtypeStruct((1, width), jnp.float32),
        ),
        in_specs=[pl.BlockSpec(memory_space=pltpu.SMEM), anywhere, anywhere, anywhere],
        out_specs=(anywhere, pl.BlockSpec(memory_space=pltpu.VMEM)),
        scratch_shapes=[
            pltpu.VMEM(queries.shape, jnp.bfloat16),
            pltpu.VMEM((ctx, cores, 2, width, HD), jnp.bfloat16),
            pltpu.VMEM((heads, tok, 2 * HD), jnp.bfloat16),
            pltpu.VMEM((heads, tok, PLANE * tok), jnp.float32),
            pltpu.VMEM((planes, heads, tok, PLANE * tok), jnp.bfloat16),
            pltpu.VMEM((heads, tok, HD), jnp.float32),
            pltpu.VMEM((planes, heads, tok, HD), jnp.float32),
            pltpu.VMEM((heads, tok, 2 * HD), jnp.float32),
            pltpu.VMEM(queries.shape, jnp.bfloat16),
            pltpu.VMEM((tok, HD), jnp.float32),
            pltpu.VMEM((PLANE, cores, planes, 1, width), jnp.float32),
            pltpu.VMEM((partners, planes, 1, width), jnp.float32),
            pltpu.VMEM((planes, 1, width), jnp.float32),
            pltpu.VMEM((planes, 1, width), jnp.float32),
            pltpu.SemaphoreType.DMA((2 * cores + 1,)),
            pltpu.SemaphoreType.DMA((1,)),
            pltpu.SemaphoreType.DMA((partners,)),
            pltpu.SemaphoreType.DMA((partners,)),
            pltpu.SemaphoreType.DMA((planes,)),
            pltpu.SemaphoreType.DMA((planes,)),
        ]
        + gather_sems(planes, cores),
        compiler_params=pltpu.CompilerParams(
            collective_id=0, has_side_effects=True, vmem_limit_bytes=62 * 1024 * 1024
        ),
        name="attend",
    )(doc_lengths, queries, keys, values)
    return rows, scores.reshape(width)


def solution(mesh):
    planes, cores = mesh.shape["ctx"] // PLANE, mesh.shape["head"]
    return jax.shard_map(
        functools.partial(body, planes, cores),
        mesh=mesh,
        in_specs=(P("ctx", "head"), P("ctx", None), P("ctx", None), P()),
        out_specs=(P("ctx", "head"), P(("ctx", "head"))),
        check_vma=False,
    )
```

```python
import functools
import math

import jax
import jax.numpy as jnp
from jax import lax
from jax.experimental import pallas as pl
from jax.experimental.pallas import tpu as pltpu
from jax.sharding import PartitionSpec as P

HD = 128
HEADS = 8
PLANE = 4
BIG = 32768.0
MESH = pl.DeviceIdType.MESH
SCALE = math.log2(math.e) / math.sqrt(HD)


def place(planes):
    me, core = lax.axis_index("ctx"), lax.axis_index("head")
    return me, core, me // PLANE, me % PLANE


def remote(src, dst, send, recv, ctx, core):
    return pltpu.make_async_remote_copy(
        src_ref=src,
        dst_ref=dst,
        send_sem=send,
        recv_sem=recv,
        device_id={"ctx": ctx, "head": core},
        device_id_type=MESH,
    )


class Gather:
    def __init__(self, planes, cores, kv, send, recv, sib_send, sib_recv):
        self.planes, self.cores, self.kv = planes, cores, kv
        self.send, self.recv = send, recv
        self.sib_send, self.sib_recv = sib_send, sib_recv
        self.me, self.core, self.z, self.p = place(planes)
        self.px = self.p + 1 - 2 * (self.p % 2)
        self.py = (self.p + 2) % PLANE
        self.pd = (self.px + 2) % PLANE
        self.xn = self.z * PLANE + self.px
        self.yn = self.z * PLANE + self.py

    def block(self, s, which):
        return (self.z - s) * PLANE + (self.p, self.px, self.py, self.pd)[which]

    def ref(self, s, kind, core):
        if kind < 3:
            return self.kv.at[self.block(s, kind), core]
        return self.kv.at[self.block(s, 3), core, 4 - kind]

    def chain_copy(self, s):
        ref = self.ref(s, 0, self.core)
        return remote(ref, ref, self.send.at[0, s], self.recv.at[0, s + 1], self.me + PLANE, self.core)

    def plane_copy(self, s, kind):
        ref = self.ref(s, 0, self.core)
        if kind == 3:
            ref = self.kv.at[self.block(s, 1), self.core, 1]
        if kind == 4:
            ref = self.kv.at[self.block(s, 2), self.core, 0]
        to = self.xn if kind in (1, 4) else self.yn
        return remote(ref, ref, self.send.at[kind, s], self.recv.at[kind, s], to, self.core)

    def sib_copy(self, s, kind, step):
        ref = self.ref(s, kind, self.core)
        return remote(
            ref,
            ref,
            self.sib_send.at[kind, step - 1, s],
            self.sib_recv.at[kind, step - 1, s],
            self.me,
            (self.core + step) % self.cores,
        )

    def wait_arrival(self, s, kind):
        ref = self.ref(s, kind, self.core)
        remote(ref, ref, self.send.at[kind, s], self.recv.at[kind, s], self.xn, self.core).wait_recv()

    def sibs(self, s, kind):
        for step in range(1, self.cores):
            self.sib_copy(s, kind, step).start()

    def chain(self, s, own=False):
        if s >= self.planes:
            return

        @pl.when(s <= self.z)
        def _():
            if not own:
                self.wait_arrival(s, 0)
            if s < self.planes - 1:
                pl.when(self.z < self.planes - 1)(lambda: self.chain_copy(s).start())
            self.plane_copy(s, 1).start()
            self.plane_copy(s, 2).start()
            if not own:
                self.sibs(s, 0)

    def cross(self, s):
        if s >= self.planes:
            return

        @pl.when(s <= self.z)
        def _():
            self.wait_arrival(s, 1)
            self.plane_copy(s, 3).start()
            self.sibs(s, 1)
            self.wait_arrival(s, 2)
            self.plane_copy(s, 4).start()
            self.sibs(s, 2)

    def diagonal(self, s):
        if s >= self.planes:
            return

        @pl.when(s <= self.z)
        def _():
            for kind in (4, 3):
                self.wait_arrival(s, kind)
                self.sibs(s, kind)

    def landed(self, s, kind):
        for step in range(1, self.cores):
            ref = self.ref(s, kind, (self.core + self.cores - step) % self.cores)
            remote(
                ref,
                ref,
                self.sib_send.at[kind, step - 1, s],
                self.sib_recv.at[kind, step - 1, s],
                self.me,
                (self.core + step) % self.cores,
            ).wait_recv()

    def sent(self, s, own=False):
        pl.when(self.z < self.planes - 1)(lambda: self.chain_copy(s).wait_send())
        for kind in range(5):
            if kind > 0:
                self.plane_copy(s, kind).wait_send()
            if kind > 0 or not own:
                for step in range(1, self.cores):
                    self.sib_copy(s, kind, step).wait_send()


def gather_sems(planes, cores):
    return [
        pltpu.SemaphoreType.DMA((5, planes)),
        pltpu.SemaphoreType.DMA((5, planes)),
        pltpu.SemaphoreType.DMA((5, max(cores - 1, 1), planes)),
        pltpu.SemaphoreType.DMA((5, max(cores - 1, 1), planes)),
    ]


def doc_of(ends, start, shape):
    position = start + lax.broadcasted_iota(jnp.int32, shape, 0)
    result = jnp.zeros(shape, jnp.int32)
    for end in ends:
        result += (position >= end).astype(jnp.int32)
    return result


def kernel(planes, cores, docs_ref, q_hbm, k_hbm, v_hbm, rows_hbm, out_ref, *scratch):
    q_ref, kv, qx, s_ref, p_ref, mx_ref, m_ref, acc, o_ref, comb, cols_ref, held, mid, late = scratch[:14]
    load, store, send, recv, zsend, zrecv = scratch[14:20]
    g = Gather(planes, cores, kv, *scratch[20:])
    me, core, z, p = g.me, g.core, g.z, g.p
    tok, heads = q_ref.shape[0], q_ref.shape[1] // HD
    width = tok // cores
    span = PLANE * tok
    steps = [(a, c) for a in range(PLANE) for c in range(cores) if (a, c) != (0, 0)]

    loads = [pltpu.make_async_copy(q_hbm, q_ref, load.at[2 * cores])]
    for part in range(cores):
        rows = pl.ds(part * width, width)
        loads.append(pltpu.make_async_copy(k_hbm.at[rows], kv.at[me, part, 0], load.at[2 * part]))
        loads.append(pltpu.make_async_copy(v_hbm.at[rows], kv.at[me, part, 1], load.at[2 * part + 1]))
    for copy in loads[1:] + loads[:1]:
        copy.start()

    sem = pltpu.get_barrier_semaphore()

    def tell(ctx, to):
        pl.semaphore_signal(sem, inc=1, device_id={"ctx": ctx, "head": to}, device_id_type=MESH)

    for a, c in steps:
        tell(z * PLANE + (p + a) % PLANE, (core + c) % cores)
    for step in range(1, planes):
        tell((z + step) % planes * PLANE + p, core)
    for copy in loads[1:]:
        copy.wait()
    pl.semaphore_wait(sem, len(steps) + planes - 1)
    g.chain(0, own=True)

    ends, total = [], 0
    for i in range(docs_ref.shape[0]):
        total = total + docs_ref[i]
        ends.append(total)
    lane = lax.broadcasted_iota(jnp.int32, (tok, HD), 1)
    mark = jnp.where(lane == doc_of(ends, me * tok, (tok, HD)), 1.0, 0.0).astype(jnp.bfloat16)
    loads[0].wait()
    for h in range(heads):
        qx[h, :, :HD] = q_ref[:, h * HD : (h + 1) * HD]
        qx[h, :, HD:] = mark
    cols_ref[...] = jnp.zeros_like(cols_ref)
    comb[...] = jnp.zeros_like(comb)
    ones = jnp.ones((tok, HD), jnp.bfloat16)
    row = lax.broadcasted_iota(jnp.int32, (tok, tok), 0)
    col = lax.broadcasted_iota(jnp.int32, (tok, tok), 1)

    def whole(b, which):
        return jnp.concatenate([kv[b, c, which] for c in range(cores)], axis=0)

    def scan(s, which, own):
        b = g.block(s, which)
        bar = jnp.where(lane == doc_of(ends, b * tok, (tok, HD)), 0.0, -BIG).astype(jnp.bfloat16)
        kx = jnp.concatenate([whole(b, 0), bar], axis=1)
        for h in range(heads):
            x = lax.dot_general(qx[h], kx, (((1,), (1,)), ((), ())), preferred_element_type=jnp.float32)
            if own:
                x = jnp.where(col + (b - me) * tok <= row, x, -BIG)
            s_ref[s % 2, h, :, which * tok : (which + 1) * tok] = x
            top = x[:, :HD]
            for i in range(1, tok // HD):
                top = jnp.maximum(top, x[:, i * HD : (i + 1) * HD])
            mx_ref[s % 2, h] = top if which == 0 else jnp.maximum(mx_ref[s % 2, h], top)

    def weigh(s, h):
        top = jnp.broadcast_to(jnp.max(mx_ref[s % 2, h], axis=1, keepdims=True) * SCALE, (tok, HD))
        if s > 0:
            old = m_ref[s - 1, h]
            top = jnp.maximum(old, top)
            fade = jnp.exp2(old - top)
        m_ref[s, h] = top
        wide = jnp.concatenate([top] * (tok // HD), axis=1)
        for which in range(PLANE):
            part = slice(which * tok, (which + 1) * tok)
            p_ref[s, h, :, part] = jnp.exp2(s_ref[s % 2, h, :, part] * SCALE - wide).astype(jnp.bfloat16)
        vx = jnp.concatenate(
            [jnp.concatenate([whole(g.block(s, which), 1), ones], axis=1) for which in range(PLANE)], axis=0
        )
        new = jnp.dot(p_ref[s, h], vx, preferred_element_type=jnp.float32)
        if s > 0:
            new += acc[h] * jnp.concatenate([fade, fade], axis=1)
        acc[h] = new

    def step(s, which):
        scan(s, which, s == 0)
        if s > 0:
            for h in range(which, heads, PLANE):
                weigh(s - 1, h)

    def one_round(s):
        if s > 0:
            g.landed(s, 0)
            step(s, 0)
        g.landed(s, 1)
        step(s, 1)
        g.chain(s + 2)
        g.landed(s, 2)
        step(s, 2)
        g.cross(s + 1)
        g.landed(s, 4)
        g.landed(s, 3)
        step(s, 3)
        g.diagonal(s + 1)

    step(0, 0)
    g.chain(1)
    g.cross(0)
    g.diagonal(0)
    one_round(0)
    for s in range(1, planes):
        pl.when(s <= z)(functools.partial(one_round, s))
    for s in range(planes):

        @pl.when(s == z)
        def _():
            for h in range(heads):
                weigh(s, h)

    for h in range(heads):
        inverse = 1.0 / acc[h, :, HD:]
        o_ref[:, h * HD : (h + 1) * HD] = (acc[h, :, :HD] * inverse).astype(o_ref.dtype)
        acc[h, :, HD:] = inverse

    @pl.loop(0, z + 1)
    def _(s):
        for h in range(heads):
            weight = jnp.exp2(m_ref[s, h] - m_ref[z, h]) * acc[h, :, HD:]
            comb[...] = jnp.where(lane == s * heads + h, weight, comb[...])

    out_copy = pltpu.make_async_copy(o_ref, rows_hbm, store.at[0])
    out_copy.start()
    across = jnp.transpose(comb[...])
    held_rows = mx_ref.at[0]
    for half in range(tok // HD):
        held_rows[0, half * HD : (half + 1) * HD, :] = across[:, half * HD : (half + 1) * HD]
    line = lax.broadcasted_iota(jnp.int32, (16, tok), 0)

    @pl.loop(0, z + 1)
    def _(s):
        sums = jnp.zeros((16, span), jnp.float32)
        for h in range(heads):
            w = jnp.concatenate(
                [held_rows[0, pl.ds(half * HD + s * heads + h, 1), :] for half in range(tok // HD)], axis=1
            )
            w = jnp.broadcast_to(w, (16, tok))
            high = w.astype(jnp.bfloat16).astype(jnp.float32)
            w = jnp.where(line == 0, high, jnp.where(line == 1, w - high, 0.0)).astype(jnp.bfloat16)
            sums += jnp.dot(w, p_ref[s, h], preferred_element_type=jnp.float32)
        sums = jnp.sum(sums, axis=0, keepdims=True)
        for which in range(PLANE):
            b = g.block(s, which)
            for c in range(cores):
                start = which * tok + c * width
                cols_ref[b % PLANE, c, b // PLANE] = sums[:, start : start + width]

    def plane_copy(n):
        a, c = steps[n]
        pn, cn = (p + a) % PLANE, (core + c) % cores
        return remote(cols_ref.at[pn, cn], held.at[n], send.at[n], recv.at[n], z * PLANE + pn, cn)

    for n in range(len(steps)):
        plane_copy(n).start()
    g.sent(0, own=True)

    @pl.loop(1, z + 1)
    def _(s):
        g.sent(s)

    total = cols_ref[p, core]
    for n in range(len(steps)):
        plane_copy(n).wait_recv()
        total += held[n]
    mid[...] = total

    def z_copy(step):
        to = (z + step) % planes
        return remote(mid.at[to], late.at[step], zsend.at[step], zrecv.at[step], to * PLANE + p, core)

    for step in range(1, planes):
        z_copy(step).start()
    result = mid[z]
    for step in range(1, planes):
        z_copy(step).wait_recv()
        result += late[step]
    out_ref[...] = result * (1.0 / HEADS)
    for n in range(len(steps)):
        plane_copy(n).wait_send()
    for step in range(1, planes):
        z_copy(step).wait_send()
    out_copy.wait()


def body(planes, cores, queries, keys, values, doc_lengths):
    tok, heads = queries.shape[0], queries.shape[1] // HD
    ctx, width = planes * PLANE, tok // cores
    partners = PLANE * cores - 1
    anywhere = pl.BlockSpec(memory_space=pl.ANY)
    rows, scores = pl.pallas_call(
        functools.partial(kernel, planes, cores),
        out_shape=(
            jax.ShapeDtypeStruct(queries.shape, jnp.bfloat16),
            jax.ShapeDtypeStruct((1, width), jnp.float32),
        ),
        in_specs=[pl.BlockSpec(memory_space=pltpu.SMEM), anywhere, anywhere, anywhere],
        out_specs=(anywhere, pl.BlockSpec(memory_space=pltpu.VMEM)),
        scratch_shapes=[
            pltpu.VMEM(queries.shape, jnp.bfloat16),
            pltpu.VMEM((ctx, cores, 2, width, HD), jnp.bfloat16),
            pltpu.VMEM((heads, tok, 2 * HD), jnp.bfloat16),
            pltpu.VMEM((2, heads, tok, PLANE * tok), jnp.float32),
            pltpu.VMEM((planes, heads, tok, PLANE * tok), jnp.bfloat16),
            pltpu.VMEM((2, heads, tok, HD), jnp.float32),
            pltpu.VMEM((planes, heads, tok, HD), jnp.float32),
            pltpu.VMEM((heads, tok, 2 * HD), jnp.float32),
            pltpu.VMEM(queries.shape, jnp.bfloat16),
            pltpu.VMEM((tok, HD), jnp.float32),
            pltpu.VMEM((PLANE, cores, planes, 1, width), jnp.float32),
            pltpu.VMEM((partners, planes, 1, width), jnp.float32),
            pltpu.VMEM((planes, 1, width), jnp.float32),
            pltpu.VMEM((planes, 1, width), jnp.float32),
            pltpu.SemaphoreType.DMA((2 * cores + 1,)),
            pltpu.SemaphoreType.DMA((1,)),
            pltpu.SemaphoreType.DMA((partners,)),
            pltpu.SemaphoreType.DMA((partners,)),
            pltpu.SemaphoreType.DMA((planes,)),
            pltpu.SemaphoreType.DMA((planes,)),
        ]
        + gather_sems(planes, cores),
        compiler_params=pltpu.CompilerParams(
            collective_id=0, has_side_effects=True, vmem_limit_bytes=62 * 1024 * 1024
        ),
        name="attend",
    )(doc_lengths, queries, keys, values)
    return rows, scores.reshape(width)


def solution(mesh):
    planes, cores = mesh.shape["ctx"] // PLANE, mesh.shape["head"]
    return jax.shard_map(
        functools.partial(body, planes, cores),
        mesh=mesh,
        in_specs=(P("ctx", "head"), P("ctx", None), P("ctx", None), P()),
        out_specs=(P("ctx", "head"), P(("ctx", "head"))),
        check_vma=False,
    )
```

```python
import functools
import math

import jax
import jax.numpy as jnp
from jax import lax
from jax.experimental import pallas as pl
from jax.experimental.pallas import tpu as pltpu
from jax.sharding import PartitionSpec as P

HD = 128
HEADS = 8
PLANE = 4
BIG = 32768.0
MESH = pl.DeviceIdType.MESH
SCALE = math.log2(math.e) / math.sqrt(HD)


def place(planes):
    me, core = lax.axis_index("ctx"), lax.axis_index("head")
    return me, core, me // PLANE, me % PLANE


def remote(src, dst, send, recv, ctx, core):
    return pltpu.make_async_remote_copy(
        src_ref=src,
        dst_ref=dst,
        send_sem=send,
        recv_sem=recv,
        device_id={"ctx": ctx, "head": core},
        device_id_type=MESH,
    )


class Gather:
    def __init__(self, planes, cores, kv, send, recv, sib_send, sib_recv):
        self.planes, self.cores, self.kv = planes, cores, kv
        self.send, self.recv = send, recv
        self.sib_send, self.sib_recv = sib_send, sib_recv
        self.me, self.core, self.z, self.p = place(planes)
        self.px = self.p + 1 - 2 * (self.p % 2)
        self.py = (self.p + 2) % PLANE
        self.pd = (self.px + 2) % PLANE
        self.xn = self.z * PLANE + self.px
        self.yn = self.z * PLANE + self.py

    def block(self, s, which):
        return (self.z - s) * PLANE + (self.p, self.px, self.py, self.pd)[which]

    def ref(self, s, kind, core):
        if kind < 3:
            return self.kv.at[self.block(s, kind), core]
        return self.kv.at[self.block(s, 3), core, 4 - kind]

    def chain_copy(self, s):
        ref = self.ref(s, 0, self.core)
        return remote(ref, ref, self.send.at[0, s], self.recv.at[0, s + 1], self.me + PLANE, self.core)

    def plane_copy(self, s, kind):
        ref = self.ref(s, 0, self.core)
        if kind == 3:
            ref = self.kv.at[self.block(s, 1), self.core, 1]
        if kind == 4:
            ref = self.kv.at[self.block(s, 2), self.core, 0]
        to = self.xn if kind in (1, 4) else self.yn
        return remote(ref, ref, self.send.at[kind, s], self.recv.at[kind, s], to, self.core)

    def sib_copy(self, s, kind, step):
        ref = self.ref(s, kind, self.core)
        return remote(
            ref,
            ref,
            self.sib_send.at[kind, step - 1, s],
            self.sib_recv.at[kind, step - 1, s],
            self.me,
            (self.core + step) % self.cores,
        )

    def wait_arrival(self, s, kind):
        ref = self.ref(s, kind, self.core)
        remote(ref, ref, self.send.at[kind, s], self.recv.at[kind, s], self.xn, self.core).wait_recv()

    def sibs(self, s, kind):
        for step in range(1, self.cores):
            self.sib_copy(s, kind, step).start()

    def chain(self, s, own=False):
        if s >= self.planes:
            return

        @pl.when(s <= self.z)
        def _():
            if not own:
                self.wait_arrival(s, 0)
            if s < self.planes - 1:
                pl.when(self.z < self.planes - 1)(lambda: self.chain_copy(s).start())
            self.plane_copy(s, 1).start()
            self.plane_copy(s, 2).start()
            if not own:
                self.sibs(s, 0)

    def cross(self, s):
        if s >= self.planes:
            return

        @pl.when(s <= self.z)
        def _():
            self.wait_arrival(s, 1)
            self.plane_copy(s, 3).start()
            self.sibs(s, 1)
            self.wait_arrival(s, 2)
            self.plane_copy(s, 4).start()
            self.sibs(s, 2)

    def diagonal(self, s):
        if s >= self.planes:
            return

        @pl.when(s <= self.z)
        def _():
            for kind in (4, 3):
                self.wait_arrival(s, kind)
                self.sibs(s, kind)

    def landed(self, s, kind):
        for step in range(1, self.cores):
            ref = self.ref(s, kind, (self.core + self.cores - step) % self.cores)
            remote(
                ref,
                ref,
                self.sib_send.at[kind, step - 1, s],
                self.sib_recv.at[kind, step - 1, s],
                self.me,
                (self.core + step) % self.cores,
            ).wait_recv()

    def sent(self, s, own=False):
        pl.when(self.z < self.planes - 1)(lambda: self.chain_copy(s).wait_send())
        for kind in range(5):
            if kind > 0:
                self.plane_copy(s, kind).wait_send()
            if kind > 0 or not own:
                for step in range(1, self.cores):
                    self.sib_copy(s, kind, step).wait_send()


def gather_sems(planes, cores):
    return [
        pltpu.SemaphoreType.DMA((5, planes)),
        pltpu.SemaphoreType.DMA((5, planes)),
        pltpu.SemaphoreType.DMA((5, max(cores - 1, 1), planes)),
        pltpu.SemaphoreType.DMA((5, max(cores - 1, 1), planes)),
    ]


def doc_of(ends, start, shape):
    position = start + lax.broadcasted_iota(jnp.int32, shape, 0)
    result = jnp.zeros(shape, jnp.int32)
    for end in ends:
        result += (position >= end).astype(jnp.int32)
    return result


def kernel(planes, cores, docs_ref, q_hbm, k_hbm, v_hbm, rows_hbm, out_ref, *scratch):
    q_ref, kv, qx, s_ref, p_ref, mx_ref, m_ref, acc, o_ref, comb, cols_ref, held, mid, late = scratch[:14]
    load, store, send, recv, zsend, zrecv = scratch[14:20]
    g = Gather(planes, cores, kv, *scratch[20:])
    me, core, z, p = g.me, g.core, g.z, g.p
    tok, heads = q_ref.shape[0], q_ref.shape[1] // HD
    width = tok // cores
    span = PLANE * tok
    steps = [(a, c) for a in range(PLANE) for c in range(cores) if (a, c) != (0, 0)]

    loads = [pltpu.make_async_copy(q_hbm, q_ref, load.at[2 * cores])]
    for part in range(cores):
        rows = pl.ds(part * width, width)
        loads.append(pltpu.make_async_copy(k_hbm.at[rows], kv.at[me, part, 0], load.at[2 * part]))
        loads.append(pltpu.make_async_copy(v_hbm.at[rows], kv.at[me, part, 1], load.at[2 * part + 1]))
    for copy in loads[1:] + loads[:1]:
        copy.start()

    sem = pltpu.get_barrier_semaphore()

    def tell(ctx, to):
        pl.semaphore_signal(sem, inc=1, device_id={"ctx": ctx, "head": to}, device_id_type=MESH)

    for a, c in steps:
        tell(z * PLANE + (p + a) % PLANE, (core + c) % cores)
    for step in range(1, planes):
        tell((z + step) % planes * PLANE + p, core)
    for copy in loads[1:]:
        copy.wait()
    pl.semaphore_wait(sem, len(steps) + planes - 1)
    g.chain(0, own=True)

    ends, total = [], 0
    for i in range(docs_ref.shape[0]):
        total = total + docs_ref[i]
        ends.append(total)
    lane = lax.broadcasted_iota(jnp.int32, (tok, HD), 1)
    mark = jnp.where(lane == doc_of(ends, me * tok, (tok, HD)), 1.0, 0.0).astype(jnp.bfloat16)
    loads[0].wait()
    for h in range(heads):
        qx[h, :, :HD] = q_ref[:, h * HD : (h + 1) * HD]
        qx[h, :, HD:] = mark
    cols_ref[...] = jnp.zeros_like(cols_ref)
    comb[...] = jnp.zeros_like(comb)
    ones = jnp.ones((tok, HD), jnp.bfloat16)
    row = lax.broadcasted_iota(jnp.int32, (tok, tok), 0)
    col = lax.broadcasted_iota(jnp.int32, (tok, tok), 1)

    def whole(b, which):
        return jnp.concatenate([kv[b, c, which] for c in range(cores)], axis=0)

    def scan(s, which, own):
        b = g.block(s, which)
        bar = jnp.where(lane == doc_of(ends, b * tok, (tok, HD)), 0.0, -BIG).astype(jnp.bfloat16)
        kx = jnp.concatenate([whole(b, 0), bar], axis=1)
        for h in range(heads):
            x = lax.dot_general(qx[h], kx, (((1,), (1,)), ((), ())), preferred_element_type=jnp.float32)
            if own:
                x = jnp.where(col + (b - me) * tok <= row, x, -BIG)
            s_ref[s % 2, h, :, which * tok : (which + 1) * tok] = x
            top = x[:, :HD]
            for i in range(1, tok // HD):
                top = jnp.maximum(top, x[:, i * HD : (i + 1) * HD])
            mx_ref[s % 2, h] = top if which == 0 else jnp.maximum(mx_ref[s % 2, h], top)

    def weigh(s, h):
        top = jnp.broadcast_to(jnp.max(mx_ref[s % 2, h], axis=1, keepdims=True) * SCALE, (tok, HD))
        if s > 0:
            old = m_ref[s - 1, h]
            top = jnp.maximum(old, top)
            fade = jnp.exp2(old - top)
        m_ref[s, h] = top
        wide = jnp.concatenate([top] * (tok // HD), axis=1)
        for which in range(PLANE):
            part = slice(which * tok, (which + 1) * tok)
            p_ref[s, h, :, part] = jnp.exp2(s_ref[s % 2, h, :, part] * SCALE - wide).astype(jnp.bfloat16)
        vx = jnp.concatenate(
            [jnp.concatenate([whole(g.block(s, which), 1), ones], axis=1) for which in range(PLANE)], axis=0
        )
        new = jnp.dot(p_ref[s, h], vx, preferred_element_type=jnp.float32)
        if s > 0:
            new += acc[h] * jnp.concatenate([fade, fade], axis=1)
        acc[h] = new

    def step(s, which):
        scan(s, which, s == 0)
        if s > 0:
            for h in range(which, heads, PLANE):
                weigh(s - 1, h)

    def one_round(s):
        if s > 0:
            g.landed(s, 0)
            step(s, 0)
        g.landed(s, 1)
        step(s, 1)
        g.chain(s + 3)
        g.landed(s, 2)
        step(s, 2)
        g.cross(s + 2)
        g.landed(s, 4)
        g.landed(s, 3)
        step(s, 3)
        g.diagonal(s + 1)

    step(0, 0)
    g.chain(1)
    g.cross(0)
    g.chain(2)
    g.cross(1)
    g.diagonal(0)
    one_round(0)
    for s in range(1, planes):
        pl.when(s <= z)(functools.partial(one_round, s))
    for s in range(planes):

        @pl.when(s == z)
        def _():
            for h in range(heads):
                weigh(s, h)

    for h in range(heads):
        inverse = 1.0 / acc[h, :, HD:]
        o_ref[:, h * HD : (h + 1) * HD] = (acc[h, :, :HD] * inverse).astype(o_ref.dtype)
        acc[h, :, HD:] = inverse

    @pl.loop(0, z + 1)
    def _(s):
        for h in range(heads):
            weight = jnp.exp2(m_ref[s, h] - m_ref[z, h]) * acc[h, :, HD:]
            comb[...] = jnp.where(lane == s * heads + h, weight, comb[...])

    out_copy = pltpu.make_async_copy(o_ref, rows_hbm, store.at[0])
    out_copy.start()
    across = jnp.transpose(comb[...])
    held_rows = mx_ref.at[0]
    for half in range(tok // HD):
        held_rows[0, half * HD : (half + 1) * HD, :] = across[:, half * HD : (half + 1) * HD]
    line = lax.broadcasted_iota(jnp.int32, (16, tok), 0)

    @pl.loop(0, z + 1)
    def _(s):
        sums = jnp.zeros((16, span), jnp.float32)
        for h in range(heads):
            w = jnp.concatenate(
                [held_rows[0, pl.ds(half * HD + s * heads + h, 1), :] for half in range(tok // HD)], axis=1
            )
            w = jnp.broadcast_to(w, (16, tok))
            high = w.astype(jnp.bfloat16).astype(jnp.float32)
            w = jnp.where(line == 0, high, jnp.where(line == 1, w - high, 0.0)).astype(jnp.bfloat16)
            sums += jnp.dot(w, p_ref[s, h], preferred_element_type=jnp.float32)
        sums = jnp.sum(sums, axis=0, keepdims=True)
        for which in range(PLANE):
            b = g.block(s, which)
            for c in range(cores):
                start = which * tok + c * width
                cols_ref[b % PLANE, c, b // PLANE] = sums[:, start : start + width]

    def plane_copy(n):
        a, c = steps[n]
        pn, cn = (p + a) % PLANE, (core + c) % cores
        return remote(cols_ref.at[pn, cn], held.at[n], send.at[n], recv.at[n], z * PLANE + pn, cn)

    for n in range(len(steps)):
        plane_copy(n).start()
    g.sent(0, own=True)

    @pl.loop(1, z + 1)
    def _(s):
        g.sent(s)

    total = cols_ref[p, core]
    for n in range(len(steps)):
        plane_copy(n).wait_recv()
        total += held[n]
    mid[...] = total

    def z_copy(step):
        to = (z + step) % planes
        return remote(mid.at[to], late.at[step], zsend.at[step], zrecv.at[step], to * PLANE + p, core)

    for step in range(1, planes):
        z_copy(step).start()
    result = mid[z]
    for step in range(1, planes):
        z_copy(step).wait_recv()
        result += late[step]
    out_ref[...] = result * (1.0 / HEADS)
    for n in range(len(steps)):
        plane_copy(n).wait_send()
    for step in range(1, planes):
        z_copy(step).wait_send()
    out_copy.wait()


def body(planes, cores, queries, keys, values, doc_lengths):
    tok, heads = queries.shape[0], queries.shape[1] // HD
    ctx, width = planes * PLANE, tok // cores
    partners = PLANE * cores - 1
    anywhere = pl.BlockSpec(memory_space=pl.ANY)
    rows, scores = pl.pallas_call(
        functools.partial(kernel, planes, cores),
        out_shape=(
            jax.ShapeDtypeStruct(queries.shape, jnp.bfloat16),
            jax.ShapeDtypeStruct((1, width), jnp.float32),
        ),
        in_specs=[pl.BlockSpec(memory_space=pltpu.SMEM), anywhere, anywhere, anywhere],
        out_specs=(anywhere, pl.BlockSpec(memory_space=pltpu.VMEM)),
        scratch_shapes=[
            pltpu.VMEM(queries.shape, jnp.bfloat16),
            pltpu.VMEM((ctx, cores, 2, width, HD), jnp.bfloat16),
            pltpu.VMEM((heads, tok, 2 * HD), jnp.bfloat16),
            pltpu.VMEM((2, heads, tok, PLANE * tok), jnp.float32),
            pltpu.VMEM((planes, heads, tok, PLANE * tok), jnp.bfloat16),
            pltpu.VMEM((2, heads, tok, HD), jnp.float32),
            pltpu.VMEM((planes, heads, tok, HD), jnp.float32),
            pltpu.VMEM((heads, tok, 2 * HD), jnp.float32),
            pltpu.VMEM(queries.shape, jnp.bfloat16),
            pltpu.VMEM((tok, HD), jnp.float32),
            pltpu.VMEM((PLANE, cores, planes, 1, width), jnp.float32),
            pltpu.VMEM((partners, planes, 1, width), jnp.float32),
            pltpu.VMEM((planes, 1, width), jnp.float32),
            pltpu.VMEM((planes, 1, width), jnp.float32),
            pltpu.SemaphoreType.DMA((2 * cores + 1,)),
            pltpu.SemaphoreType.DMA((1,)),
            pltpu.SemaphoreType.DMA((partners,)),
            pltpu.SemaphoreType.DMA((partners,)),
            pltpu.SemaphoreType.DMA((planes,)),
            pltpu.SemaphoreType.DMA((planes,)),
        ]
        + gather_sems(planes, cores),
        compiler_params=pltpu.CompilerParams(
            collective_id=0, has_side_effects=True, vmem_limit_bytes=62 * 1024 * 1024
        ),
        name="attend",
    )(doc_lengths, queries, keys, values)
    return rows, scores.reshape(width)


def solution(mesh):
    planes, cores = mesh.shape["ctx"] // PLANE, mesh.shape["head"]
    return jax.shard_map(
        functools.partial(body, planes, cores),
        mesh=mesh,
        in_specs=(P("ctx", "head"), P("ctx", None), P("ctx", None), P()),
        out_specs=(P("ctx", "head"), P(("ctx", "head"))),
        check_vma=False,
    )
```
